32 devices in a mesh: dp: 4 (over x, core), sx: 2 (over y), sy: 4 (over z).
Axes of the slice: x: 2, y: 2, z: 4, core: 2. Of those that a mesh axis runs over, the one named last changes fastest.
Arguments:
- volume: bfloat16 [4, 32, 64, 32, 128], P('dp', 'sx', 'sy'), may hold values from -6 to 6
- block_active: int32 [4, 2, 4, 2], P('dp', 'sx', 'sy'), may hold values from 0 to 1, as said below
- weight: bfloat16 [3, 3, 3, 128, 128], replicated, may hold values from -0.109375 to 0.109375
- bias: float32 [128], replicated, may hold values from -3 to 3
- cotangent: bfloat16 [4, 32, 64, 32, 128], P('dp', 'sx', 'sy'), may hold values from -0.01171875 to 0.01171875
Outputs:
- activated: bfloat16 [4, 32, 64, 32, 128], P('dp', 'sx', 'sy')
- grad_weight: float32 [3, 3, 3, 128, 128], replicated
- grad_bias: float32 [128], replicated
The draws below stay inside these ranges and needn't reach their ends.
Inputs may be any that keep to these rules, and one draw needn't show every extreme that they name: `block_active`: every tile of 2 blocks along depth (one value of the first three indices) has at least one active block; the number of active blocks of a tile is drawn evenly from 1 to 2.
All inputs are finite; a program needn't handle non-finite values.
Results may differ from the reference program's by a relative error of at most 0.006.
Values may be sent and summed in bfloat16 or wider, within the bound.
A program may use at most 64 MiB of HBM per device.

```python
import jax
import jax.numpy as jnp
from jax import lax

C = 128
BLK = 16
TB = 2
CROPS = 4
NBX = 2
NBY = 4
NX = 32
NY = 64
NZ = 32


def draw_block_active(key, part):
    key_count, key_order = jax.random.split(key)
    counts = jax.random.randint(key_count, (CROPS, NBX, NBY, 1), 1, TB + 1)
    scores = jax.random.randint(key_order, (CROPS, NBX, NBY, TB), 0, 1 << 20) * TB + jnp.arange(TB, dtype=jnp.int32)
    ranks = jnp.argsort(jnp.argsort(scores, axis=-1), axis=-1)
    return (ranks < counts).astype(jnp.int32)


def shard_levels(own_key, dims, shards, least, top_value):
    gain = 1.0
    for axis_at, shards_of in shards:
        heights = jax.random.uniform(jax.random.fold_in(jax.random.fold_in(own_key, 6), axis_at), (shards_of,), jnp.float32, least / len(shards), top_value / len(shards))
        gain = gain * jnp.repeat(jnp.exp(heights), dims[axis_at] // shards_of).reshape((-1,) + (1,) * (len(dims) - 1 - axis_at))
    return gain


def centred(own_key, extent, width, most, cuts=(), kind=jnp.bfloat16):
    entries = jax.random.normal(own_key, extent, jnp.float32) * width
    if len(cuts) > 0:
        entries = shard_levels(own_key, extent, cuts, -0.22, 0.18) * entries
    return jnp.clip(entries, min=-most, max=most).astype(kind)


def setup_inputs(seed: int = 0) -> dict:
    key_list = jax.random.split(jax.random.key(seed), 6)
    return {
        "volume": centred(key_list[0], (CROPS, NX, NY, NZ, C), 1.0, 6.0, ((0, 4), (1, 2), (2, 4))),
        "block_active": draw_block_active(jax.random.fold_in(key_list[5], 71), 0),
        "weight": centred(key_list[2], (3, 3, 3, C, C), (27 * C) ** -0.5, 0.109375),
        "bias": centred(key_list[3], (C,), 0.5, 3.0, (), jnp.float32),
        "cotangent": centred(key_list[4], (CROPS, NX, NY, NZ, C), (CROPS * NX * NY * NZ) ** -0.5, 0.01171875, ((0, 4), (1, 2), (2, 4))),
    }


def reference(volume, block_active, weight, bias, cotangent):
    kernel = weight.astype(jnp.float32)

    def one_crop(items):
        vol, act, cot = items
        vox = jnp.repeat(jnp.repeat(jnp.repeat(act, BLK, 0), BLK, 1), BLK, 2).astype(jnp.float32)[..., None]
        masked = (vol.astype(jnp.float32) * vox)[None]
        padded = jnp.pad(masked, ((0, 0), (1, 1), (1, 1), (1, 1), (0, 0)))
        pre = lax.conv_general_dilated(padded, kernel, (1, 1, 1), "VALID", dimension_numbers=("NDHWC", "DHWIO", "NDHWC"), precision=lax.Precision.HIGHEST) + bias
        sig = jax.nn.sigmoid(pre)
        out = (pre * sig * vox[None]).astype(jnp.bfloat16)
        dpre = (cot[None].astype(jnp.float32) * sig * (1.0 + pre * (1.0 - sig)) * vox[None]).astype(jnp.bfloat16)
        dpre = lax.optimization_barrier(dpre).astype(jnp.float32)
        grads = []
        for a in range(3):
            for b in range(3):
                for c in range(3):
                    piece = padded[:, a:a + NX, b:b + NY, c:c + NZ, :]
                    grads.append(lax.dot_general(piece, dpre, (((0, 1, 2, 3), (0, 1, 2, 3)), ((), ())), precision=lax.Precision.HIGHEST))
        grad_w = jnp.stack(grads).reshape(3, 3, 3, C, C)
        grad_b = jnp.sum(dpre, axis=(0, 1, 2, 3))
        return out[0], grad_w, grad_b

    outs, grad_ws, grad_bs = lax.map(one_crop, (volume, block_active, cotangent))
    return outs, jnp.sum(grad_ws, axis=0), jnp.sum(grad_bs, axis=0)
```

```python
import functools

import jax
import jax.numpy as jnp
from jax import lax
from jax.experimental import pallas as pl
from jax.experimental.pallas import tpu as pltpu
from jax.sharding import PartitionSpec as P

MESH = pl.DeviceIdType.MESH
VM = pl.BlockSpec(memory_space=pltpu.VMEM)
SM = pl.BlockSpec(memory_space=pltpu.SMEM)
NEAR = [(dx, dy) for dx in (-1, 0, 1) for dy in (-1, 0, 1) if (dx, dy) != (0, 0)]
BF = jnp.bfloat16
F32 = jnp.float32


def depth_mask(act_ref, rows, depth, edge):
    z = lax.rem(lax.broadcasted_iota(jnp.int32, (rows, 128), 0), depth)
    m = jnp.zeros((rows, 128), F32)
    for k in range(depth // edge):
        inside = jnp.logical_and(z >= k * edge, z < (k + 1) * edge)
        m = jnp.where(inside, act_ref[k].astype(F32), m)
    return m


def halo_kernel(nsx, nsy, edge, act_ref, vol_ref, hx_ref, hy_ref, fx, fy, send, recv):
    nx, ny, nz, _ = vol_ref.shape
    ix, iy = lax.axis_index("sx"), lax.axis_index("sy")

    def there(dx, dy):
        x, y = ix + dx, iy + dy
        return (x >= 0) & (x < nsx) & (y >= 0) & (y < nsy)

    barrier = pltpu.get_barrier_semaphore()
    for dx, dy in NEAR:
        @pl.when(there(dx, dy))
        def _():
            pl.semaphore_signal(barrier, inc=1, device_id={"sx": ix + dx, "sy": iy + dy},
                                device_id_type=MESH)
    mask = depth_mask(act_ref, nz, nz, edge)[None].astype(BF)
    for side in range(2):
        fx[side] = vol_ref[side * (nx - 1)] * mask
        fy[side] = vol_ref[:, side * (ny - 1)] * mask
    pl.semaphore_wait(barrier, sum(there(dx, dy).astype(jnp.int32) for dx, dy in NEAR))

    def slot(dx, dy):
        if dy == 0:
            return hx_ref.at[int(dx > 0)]
        if dx == 0:
            return hy_ref.at[int(dy > 0), pl.ds(1, nx)]
        return hy_ref.at[int(dy > 0), (nx + 1) * int(dx > 0)]

    def copy(k):
        dx, dy = NEAR[k]
        if dy == 0:
            src = fx.at[int(dx > 0)]
        elif dx == 0:
            src = fy.at[int(dy > 0)]
        else:
            src = fx.at[int(dx > 0), (ny - 1) * int(dy > 0)]
        opp = NEAR.index((-dx, -dy))
        return pltpu.make_async_remote_copy(
            src_ref=src, dst_ref=slot(-dx, -dy), send_sem=send.at[k], recv_sem=recv.at[opp],
            device_id={"sx": ix + dx, "sy": iy + dy}, device_id_type=MESH)

    for k, (dx, dy) in enumerate(NEAR):
        @pl.when(there(dx, dy))
        def _():
            copy(k).start()

        @pl.when(jnp.logical_not(there(dx, dy)))
        def _():
            ref = slot(dx, dy)
            ref[...] = jnp.zeros(ref.shape, BF)
    for k, (dx, dy) in enumerate(NEAR):
        @pl.when(there(dx, dy))
        def _():
            copy(k).wait_send()
            copy(NEAR.index((-dx, -dy))).wait_recv()


def work_kernel(nz, edge, act_ref, vol_ref, hx_ref, hy_ref, w_ref, bias_ref, cot_ref,
                out_ref, g_ref, cols, dpt, acc):
    nx, rows, ch = vol_ref.shape
    full = rows + 2 * nz
    mask = depth_mask(act_ref, rows, nz, edge)
    maskb = mask.astype(BF)
    mid = slice(ch, 2 * ch)
    z = lax.rem(lax.broadcasted_iota(jnp.int32, (full, ch), 0), nz)
    first, last = z == 0, z == nz - 1

    cols[0, nz:nz + rows, mid] = hx_ref[0]
    cols[nx + 1, nz:nz + rows, mid] = hx_ref[1]

    @pl.loop(0, nx)
    def _(i):
        cols[i + 1, nz:nz + rows, mid] = vol_ref[i] * maskb

    @pl.loop(0, nx + 2)
    def _(i):
        cols[i, 0:nz, mid] = hy_ref[0, i]
        cols[i, nz + rows:full, mid] = hy_ref[1, i]
        v = cols[i, :, mid].astype(F32)
        cols[i, :, 0:ch] = jnp.where(first, 0.0, pltpu.roll(v, 1, 0)).astype(BF)
        cols[i, :, 2 * ch:3 * ch] = jnp.where(last, 0.0, pltpu.roll(v, full - 1, 0)).astype(BF)

    dpt[0:2 * ch, :] = jnp.zeros((2 * ch, rows), BF)
    dpt[(nx + 2) * ch:(nx + 4) * ch, :] = jnp.zeros((2 * ch, rows), BF)
    half = 6 * 3 * ch

    def pair(p, gb):
        pre = jnp.zeros((rows, 2 * ch), F32) + bias_ref[...]
        for j in range(2):
            lhs = jnp.concatenate(
                [cols[2 * p + 2 * j + t, pl.ds(b * nz, rows), :] for t in range(2) for b in range(3)], axis=1)
            pre = pre + jnp.dot(lhs, w_ref[j * half:(j + 1) * half, :], preferred_element_type=F32)
        for t in range(2):
            y = pre[:, t * ch:(t + 1) * ch]
            sig = jax.nn.sigmoid(y)
            out_ref[2 * p + t] = (y * sig * mask).astype(BF)
            d = (cot_ref[2 * p + t].astype(F32) * sig * (1.0 + y * (1.0 - sig)) * mask).astype(BF)
            gb = gb + jnp.sum(d.astype(F32), axis=0, keepdims=True)
            dpt[pl.ds(pl.multiple_of((2 * p + t + 2) * ch, ch), ch), :] = d.T
        return gb

    gb = lax.fori_loop(0, nx // 2, pair, jnp.zeros((1, ch), F32))
    acc[...] = jnp.zeros(acc.shape, F32)

    @pl.loop(0, nx + 2)
    def _(i):
        lhs = dpt[pl.ds(pl.multiple_of(i * ch, ch), 3 * ch), :]
        rhs = jnp.concatenate([cols[i, pl.ds(b * nz, rows), :] for b in range(3)], axis=1)
        acc[...] += jnp.dot(lhs, rhs, preferred_element_type=F32)

    for a in range(3):
        for q in range(9):
            g_ref[a * 9 + q] = acc[(2 - a) * ch:(3 - a) * ch, q * ch:(q + 1) * ch].T
    g_ref[27] = jnp.broadcast_to(gb, (ch, ch))


def reduce_kernel(nsx, chunks, g_ref, out_ref, s1, r1, a1, s2, r2, a2, s3, r3, s4, fin,
                  ss, rs):
    d, x, y = lax.axis_index("dp"), lax.axis_index("sx"), lax.axis_index("sy")
    h, dh = lax.rem(d, 2), d // 2
    xl, xh = lax.rem(x, 2), x // 2
    q = dh * 2 + xl
    far = nsx // 2

    def peer1():
        return {"dp": dh * 2 + 1 - h, "sx": x, "sy": y}

    def peer2(k):
        o = lax.rem(q + k, 4)
        return o, {"dp": (o // 2) * 2 + h, "sx": xh * 2 + lax.rem(o, 2), "sy": y}

    def peer3(k):
        o = lax.rem(y + k, 4)
        return o, {"dp": d, "sx": x, "sy": o}

    def peer4(k):
        o = lax.rem(xh + k, far)
        return o, {"dp": d, "sx": o * 2 + xl, "sy": y}

    peers = [peer1()] + [peer2(k)[1] for k in (1, 2, 3)] + [peer3(k)[1] for k in (1, 2, 3)]
    peers += [peer4(k)[1] for k in range(1, far)]
    barrier = pltpu.get_barrier_semaphore()
    for p in peers:
        pl.semaphore_signal(barrier, inc=1, device_id=p, device_id_type=MESH)

    def rcopy(src, dst, c, n, p):
        return pltpu.make_async_remote_copy(src_ref=src, dst_ref=dst, send_sem=ss.at[c, n],
                                            recv_sem=rs.at[c, n], device_id=p, device_id_type=MESH)

    def part(c):
        off, size = chunks[c]
        return pl.ds(off, size)

    def c1(c):
        return [rcopy(s1.at[:, part(c)], r1.at[:, part(c)], c, 0, peer1())]

    def c2(c):
        cs = []
        for k in (1, 2, 3):
            o, p = peer2(k)
            cs.append(rcopy(s2.at[o, :, part(c)], r2.at[k, :, part(c)], c, k, p))
        return cs

    def c3(c):
        cs = []
        for k in (1, 2, 3):
            o, p = peer3(k)
            cs.append(rcopy(s3.at[o, part(c)], r3.at[k, part(c)], c, 3 + k, p))
        return cs

    def c4(c):
        cs = []
        for k in range(1, far):
            o, p = peer4(k)
            cs.append(rcopy(s4.at[xh, part(c)], s4.at[xh, part(c)], c, 13 + k, p))
        return cs

    def c4in(c):
        cs = []
        for k in range(1, far):
            o, p = peer4(far - k)
            cs.append(rcopy(s4.at[xh, part(c)], s4.at[o, part(c)], c, 13 + k, p))
        return cs

    def g3(c, inn=False):
        cs = []
        for k in (1, 2, 3):
            o, p = peer3(4 - k if inn else k)
            cs.append(rcopy(fin.at[h, q, y, part(c)], fin.at[h, q, o if inn else y, part(c)], c, 6 + k, p))
        return cs

    def g2(c, inn=False):
        cs = []
        for k in (1, 2, 3):
            o, p = peer2(4 - k if inn else k)
            cs.append(rcopy(fin.at[h, q, :, part(c)], fin.at[h, o if inn else q, :, part(c)], c, 9 + k, p))
        return cs

    def g1(c, inn=False):
        return [rcopy(fin.at[h, :, :, part(c)], fin.at[1 - h if inn else h, :, :, part(c)], c, 13, peer1())]

    def start(cs):
        for r in cs:
            r.start()

    def landed(cs):
        for r in cs:
            r.wait_recv()

    def st0(c):
        s1[:, part(c)] = g_ref[1 - h, :, part(c)].astype(BF)
        if c == 0:
            pl.semaphore_wait(barrier, len(peers))
        start(c1(c))

    def st1(c):
        landed(c1(c))
        v = g_ref[h, :, part(c)] + r1[:, part(c)].astype(F32)
        v = v.reshape((4, 4) + v.shape[1:])
        a1[:, :, part(c)] = v
        s2[:, :, part(c)] = v.astype(BF)
        start(c2(c))

    def st2(c):
        landed(c2(c))
        v = a1[q, :, part(c)]
        for k in (1, 2, 3):
            v = v + r2[k, :, part(c)].astype(F32)
        a2[:, part(c)] = v
        s3[:, part(c)] = v.astype(BF)
        start(c3(c))

    def st3(c):
        landed(c3(c))
        v = a2[y, part(c)]
        for k in (1, 2, 3):
            v = v + r3[k, part(c)].astype(F32)
        if far > 1:
            s4[xh, part(c)] = v.astype(BF)
            start(c4(c))
            landed(c4in(c))
            v = s4[0, part(c)].astype(F32)
            for k in range(1, far):
                v = v + s4[k, part(c)].astype(F32)
        fin[h, q, y, part(c)] = v.astype(BF)
        start(g3(c))

    def st4(c):
        landed(g3(c, True))
        start(g2(c))

    def st5(c):
        landed(g2(c, True))
        start(g1(c))

    def st6(c):
        landed(g1(c, True))
        out_ref[:, :, :, part(c)] = fin[:, :, :, part(c)].astype(F32)

    stages = [st0, st1, st2, st3, st4, st5, st6]
    n = len(chunks)
    for t in range(n + len(stages) - 1):
        for s in reversed(range(len(stages))):
            if 0 <= t - s < n:
                stages[s](t - s)
    for c in range(n):
        for cs in (c1(c), c2(c), c3(c), c4(c), g3(c), g2(c), g1(c)):
            for r in cs:
                r.wait_send()


def local(nsx, nsy, volume, block_active, weight, bias, cotangent):
    _, nx, ny, nz, ch = volume.shape
    blocks = block_active.shape[3]
    edge = nz // blocks
    act = block_active.reshape(blocks)
    big = pltpu.CompilerParams(vmem_limit_bytes=60 * 2**20)
    hx, hy = pl.pallas_call(
        functools.partial(halo_kernel, nsx, nsy, edge),
        out_shape=(jax.ShapeDtypeStruct((2, ny, nz, ch), BF),
                   jax.ShapeDtypeStruct((2, nx + 2, nz, ch), BF)),
        in_specs=[SM, VM], out_specs=(VM, VM),
        scratch_shapes=[pltpu.VMEM((2, ny, nz, ch), BF), pltpu.VMEM((2, nx, nz, ch), BF),
                        pltpu.SemaphoreType.DMA((8,)), pltpu.SemaphoreType.DMA((8,))],
        compiler_params=pltpu.CompilerParams(collective_id=0, has_side_effects=True,
                                             vmem_limit_bytes=32 * 2**20),
        name="halo",
    )(act, volume[0])
    w = weight.reshape(3, 9 * ch, ch)
    w2 = jnp.concatenate([jnp.pad(w, ((0, 1), (0, 0), (0, 0))), jnp.pad(w, ((1, 0), (0, 0), (0, 0)))],
                         axis=-1).reshape(36 * ch, 2 * ch)
    bias2 = jnp.concatenate([bias, bias])[None]
    rows = ny * nz
    out, g = pl.pallas_call(
        functools.partial(work_kernel, nz, edge),
        out_shape=(jax.ShapeDtypeStruct((nx, rows, ch), BF),
                   jax.ShapeDtypeStruct((28, ch, ch), F32)),
        in_specs=[SM] + [VM] * 6, out_specs=(VM, VM),
        scratch_shapes=[pltpu.VMEM((nx + 2, rows + 2 * nz, 3 * ch), BF),
                        pltpu.VMEM(((nx + 4) * ch, rows), BF),
                        pltpu.VMEM((3 * ch, 9 * ch), F32)],
        compiler_params=big, name="work",
    )(act, volume.reshape(nx, rows, ch), hx.reshape(2, rows, ch), hy, w2, bias2,
      cotangent.reshape(nx, rows, ch))
    sh = 28 * ch // 32
    chunks = ((0, 48), (48, 32), (80, 32))
    total = pl.pallas_call(
        functools.partial(reduce_kernel, nsx, chunks),
        out_shape=jax.ShapeDtypeStruct((2, 4, 4, sh, ch), F32),
        in_specs=[VM], out_specs=VM,
        scratch_shapes=[pltpu.VMEM((16, sh, ch), BF), pltpu.VMEM((16, sh, ch), BF),
                        pltpu.VMEM((4, 4, sh, ch), F32), pltpu.VMEM((4, 4, sh, ch), BF),
                        pltpu.VMEM((4, 4, sh, ch), BF), pltpu.VMEM((4, sh, ch), F32),
                        pltpu.VMEM((4, sh, ch), BF), pltpu.VMEM((4, sh, ch), BF),
                        pltpu.VMEM((max(nsx // 2, 1), sh, ch), BF),
                        pltpu.VMEM((2, 4, 4, sh, ch), BF),
                        pltpu.SemaphoreType.DMA((len(chunks), 13 + max(nsx // 2, 1))),
                        pltpu.SemaphoreType.DMA((len(chunks), 13 + max(nsx // 2, 1)))],
        compiler_params=pltpu.CompilerParams(collective_id=1, has_side_effects=True,
                                             vmem_limit_bytes=32 * 2**20),
        name="reduce",
    )(g.reshape(2, 16, sh, ch)).reshape(28, ch, ch)
    return (out.reshape(volume.shape), total[:27].reshape(weight.shape), total[27, 0])


def solution(mesh):
    tile = P("dp", "sx", "sy", None, None)
    return jax.shard_map(
        functools.partial(local, mesh.shape["sx"], mesh.shape["sy"]),
        mesh=mesh,
        in_specs=(tile, P("dp", "sx", "sy", None), P(), P(), tile),
        out_specs=(tile, P(), P()),
        check_vma=False,
    )
```

```python
import functools

import jax
import jax.numpy as jnp
from jax import lax
from jax.experimental import pallas as pl
from jax.experimental.pallas import tpu as pltpu
from jax.sharding import PartitionSpec as P

MESH = pl.DeviceIdType.MESH
VM = pl.BlockSpec(memory_space=pltpu.VMEM)
SM = pl.BlockSpec(memory_space=pltpu.SMEM)
NEAR = [(dx, dy) for dx in (-1, 0, 1) for dy in (-1, 0, 1) if (dx, dy) != (0, 0)]
BF = jnp.bfloat16
F32 = jnp.float32


def depth_mask(act_ref, rows, depth, edge):
    z = lax.rem(lax.broadcasted_iota(jnp.int32, (rows, 128), 0), depth)
    m = jnp.zeros((rows, 128), F32)
    for k in range(depth // edge):
        inside = jnp.logical_and(z >= k * edge, z < (k + 1) * edge)
        m = jnp.where(inside, act_ref[k].astype(F32), m)
    return m


def layer_kernel(nsx, nsy, edge, chunks, act_ref, bias_ref, vol_ref, w_ref, cot_ref,
                 out_ref, gw_ref, gb_ref, fx, fy, hx, hy, vb, wb, cb, ob, cols, dpt, acc,
                 g_ref, s1, r1, a1, s2, r2, a2, s3, r3, s4, fin, ls, hs, hr, ss, rs):
    nx, ny, nz, ch = vol_ref.shape
    rows = ny * nz
    d, x, y = lax.axis_index("dp"), lax.axis_index("sx"), lax.axis_index("sy")

    def there(dx, dy):
        return (x + dx >= 0) & (x + dx < nsx) & (y + dy >= 0) & (y + dy < nsy)

    h, dh = lax.rem(d, 2), d // 2
    xl, xh = lax.rem(x, 2), x // 2
    q = dh * 2 + xl
    far = nsx // 2

    def peer1():
        return {"dp": dh * 2 + 1 - h, "sx": x, "sy": y}

    def peer2(k):
        o = lax.rem(q + k, 4)
        return o, {"dp": (o // 2) * 2 + h, "sx": xh * 2 + lax.rem(o, 2), "sy": y}

    def peer3(k):
        o = lax.rem(y + k, 4)
        return o, {"dp": d, "sx": x, "sy": o}

    def peer4(k):
        o = lax.rem(xh + k, far)
        return o, {"dp": d, "sx": o * 2 + xl, "sy": y}

    peers = [peer1()] + [peer2(k)[1] for k in (1, 2, 3)] + [peer3(k)[1] for k in (1, 2, 3)]
    peers += [peer4(k)[1] for k in range(1, far)]
    barrier = pltpu.get_barrier_semaphore()
    for p in peers:
        pl.semaphore_signal(barrier, inc=1, device_id=p, device_id_type=MESH)
    for dx, dy in NEAR:
        @pl.when(there(dx, dy))
        def _():
            pl.semaphore_signal(barrier, inc=1, device_id={"sx": x + dx, "sy": y + dy},
                                device_id_type=MESH)
    load = [pltpu.make_async_copy(s, t, ls.at[k]) for k, (s, t) in enumerate((
        (vol_ref.at[0], fx.at[0]), (vol_ref.at[nx - 1], fx.at[1]),
        (vol_ref.at[:, 0], fy.at[0]), (vol_ref.at[:, ny - 1], fy.at[1]),
        (vol_ref, vb), (w_ref, wb.at[pl.ds(0, 27 * ch), pl.ds(0, ch)]),
        (w_ref, wb.at[pl.ds(9 * ch, 27 * ch), pl.ds(ch, ch)]), (cot_ref, cb)))]
    for r in load:
        r.start()
    zmask = depth_mask(act_ref, nz, nz, edge)[None].astype(BF)
    mask = depth_mask(act_ref, rows, nz, edge)
    wb[0:9 * ch, ch:2 * ch] = jnp.zeros((9 * ch, ch), BF)
    wb[27 * ch:36 * ch, 0:ch] = jnp.zeros((9 * ch, ch), BF)
    dpt[0:2 * ch, :] = jnp.zeros((2 * ch, rows), BF)
    dpt[(nx + 2) * ch:(nx + 4) * ch, :] = jnp.zeros((2 * ch, rows), BF)
    for r in load[:4]:
        r.wait()
    for side in range(2):
        fx[side] = fx[side] * zmask
        fy[side] = fy[side] * zmask
    pl.semaphore_wait(barrier, len(peers) + sum(there(dx, dy).astype(jnp.int32) for dx, dy in NEAR))

    def slot(dx, dy):
        if dy == 0:
            return hx.at[int(dx > 0)]
        if dx == 0:
            return hy.at[int(dy > 0), pl.ds(1, nx)]
        return hy.at[int(dy > 0), (nx + 1) * int(dx > 0)]

    def face(k):
        dx, dy = NEAR[k]
        if dy == 0:
            src = fx.at[int(dx > 0)]
        elif dx == 0:
            src = fy.at[int(dy > 0)]
        else:
            src = fx.at[int(dx > 0), (ny - 1) * int(dy > 0)]
        opp = NEAR.index((-dx, -dy))
        return pltpu.make_async_remote_copy(
            src_ref=src, dst_ref=slot(-dx, -dy), send_sem=hs.at[k], recv_sem=hr.at[opp],
            device_id={"sx": x + dx, "sy": y + dy}, device_id_type=MESH)

    for k, (dx, dy) in enumerate(NEAR):
        @pl.when(there(dx, dy))
        def _():
            face(k).start()

        @pl.when(jnp.logical_not(there(dx, dy)))
        def _():
            ref = slot(dx, dy)
            ref[...] = jnp.zeros(ref.shape, BF)

    z = lax.rem(lax.broadcasted_iota(jnp.int32, (rows, ch), 0), nz)
    first, last = z == 0, z == nz - 1

    def shifted(i, at, v):
        n = v.shape[0]
        here = pl.ds(at, n)
        cols[i, here, ch:2 * ch] = v.astype(BF)
        cols[i, here, 0:ch] = jnp.where(first[:n], 0.0, pltpu.roll(v, 1, 0)).astype(BF)
        cols[i, here, 2 * ch:3 * ch] = jnp.where(last[:n], 0.0, pltpu.roll(v, n - 1, 0)).astype(BF)

    load[4].wait()

    @pl.loop(0, nx)
    def _(i):
        shifted(i + 1, nz, vb[i].reshape(rows, ch).astype(F32) * mask)

    for k, (dx, dy) in enumerate(NEAR):
        @pl.when(there(dx, dy))
        def _():
            face(k).wait_send()
            face(NEAR.index((-dx, -dy))).wait_recv()
    for side in range(2):
        shifted(side * (nx + 1), nz, hx[side].reshape(rows, ch).astype(F32))

    @pl.loop(0, nx + 2)
    def _(i):
        for side in range(2):
            shifted(i, side * (nz + rows), hy[side, i].astype(F32))

    for r in load[5:]:
        r.wait()
    half = 18 * ch

    def pair(p, gb):
        pre = jnp.zeros((rows, 2 * ch), F32) + bias_ref[...]
        for j in range(2):
            lhs = jnp.concatenate(
                [cols[2 * p + 2 * j + t, pl.ds(b * nz, rows), :] for t in range(2) for b in range(3)], axis=1)
            pre = pre + jnp.dot(lhs, wb[j * half:(j + 1) * half, :], preferred_element_type=F32)
        for t in range(2):
            u = pre[:, t * ch:(t + 1) * ch]
            sig = jax.nn.sigmoid(u)
            ob[2 * p + t] = (u * sig * mask).astype(BF)
            e = (cb[2 * p + t].astype(F32) * sig * (1.0 + u * (1.0 - sig)) * mask).astype(BF)
            gb = gb + jnp.sum(e.astype(F32), axis=0, keepdims=True)
            dpt[pl.ds(pl.multiple_of((2 * p + t + 2) * ch, ch), ch), :] = e.T
        return gb

    gb = lax.fori_loop(0, nx // 2, pair, jnp.zeros((1, ch), F32))
    store = pltpu.make_async_copy(ob, out_ref, ls.at[8])
    store.start()

    def grad(q0, q1, i0, i1):
        @pl.loop(i0, i1)
        def _(p):
            i = 2 * p
            lhs = jnp.concatenate(
                [dpt[pl.ds(pl.multiple_of((i + t) * ch, ch), 3 * ch), :] for t in range(2)], axis=1)
            rhs = jnp.concatenate([jnp.concatenate(
                [cols[i + t, pl.ds((o // 3) * nz, rows), (o % 3) * ch:(o % 3 + 1) * ch] for o in range(q0, q1)],
                axis=1) for t in range(2)], axis=0)
            acc[:, q0 * ch:q1 * ch] += jnp.dot(lhs, rhs, preferred_element_type=F32)

    def put(pos, tile):
        g_ref[pos % 4 // 2, pl.ds(8 * (pos % 2), 8), pos // 4] = tile.reshape(8, 16, ch)

    def tiles(q0, q1):
        for o in range(q0, q1):
            for a in range(3):
                put(o * 3 + a, acc[(2 - a) * ch:(3 - a) * ch, o * ch:(o + 1) * ch].T)

    def rcopy(src, dst, c, n, p):
        return pltpu.make_async_remote_copy(src_ref=src, dst_ref=dst, send_sem=ss.at[c, n],
                                            recv_sem=rs.at[c, n], device_id=p, device_id_type=MESH)

    def part(c):
        off, size = chunks[c]
        return pl.ds(off, size)

    def c1(c):
        return [rcopy(s1.at[:, part(c)], r1.at[:, part(c)], c, 0, peer1())]

    def c2(c):
        cs = []
        for k in (1, 2, 3):
            o, p = peer2(k)
            cs.append(rcopy(s2.at[o, :, part(c)], r2.at[k, :, part(c)], c, k, p))
        return cs

    def c3(c):
        cs = []
        for k in (1, 2, 3):
            o, p = peer3(k)
            cs.append(rcopy(s3.at[o, part(c)], r3.at[k, part(c)], c, 3 + k, p))
        return cs

    def c4(c):
        cs = []
        for k in range(1, far):
            o, p = peer4(k)
            cs.append(rcopy(s4.at[xh, part(c)], s4.at[xh, part(c)], c, 13 + k, p))
        return cs

    def c4in(c):
        cs = []
        for k in range(1, far):
            o, p = peer4(far - k)
            cs.append(rcopy(s4.at[xh, part(c)], s4.at[o, part(c)], c, 13 + k, p))
        return cs

    def g3(c, inn=False):
        cs = []
        for k in (1, 2, 3):
            o, p = peer3(4 - k if inn else k)
            cs.append(rcopy(fin.at[h, q, y, part(c)], fin.at[h, q, o if inn else y, part(c)], c, 6 + k, p))
        return cs

    def g2(c, inn=False):
        cs = []
        for k in (1, 2, 3):
            o, p = peer2(4 - k if inn else k)
            cs.append(rcopy(fin.at[h, q, :, part(c)], fin.at[h, o if inn else q, :, part(c)], c, 9 + k, p))
        return cs

    def g1(c, inn=False):
        return [rcopy(fin.at[h, :, :, part(c)], fin.at[1 - h if inn else h, :, :, part(c)], c, 13, peer1())]

    def start(cs):
        for r in cs:
            r.start()

    def landed(cs):
        for r in cs:
            r.wait_recv()

    def st0(c):
        s1[:, part(c)] = g_ref[1 - h, :, part(c)].astype(BF)
        start(c1(c))

    def st1(c):
        landed(c1(c))
        v = g_ref[h, :, part(c)] + r1[:, part(c)].astype(F32)
        v = v.reshape((4, 4) + v.shape[1:])
        a1[:, :, part(c)] = v
        s2[:, :, part(c)] = v.astype(BF)
        start(c2(c))

    def st2(c):
        landed(c2(c))
        v = a1[q, :, part(c)]
        for k in (1, 2, 3):
            v = v + r2[k, :, part(c)].astype(F32)
        a2[:, part(c)] = v
        s3[:, part(c)] = v.astype(BF)
        start(c3(c))

    def st3(c):
        landed(c3(c))
        v = a2[y, part(c)]
        for k in (1, 2, 3):
            v = v + r3[k, part(c)].astype(F32)
        if far > 1:
            s4[xh, part(c)] = v.astype(BF)
            start(c4(c))
            landed(c4in(c))
            v = s4[0, part(c)].astype(F32)
            for k in range(1, far):
                v = v + s4[k, part(c)].astype(F32)
        fin[h, q, y, part(c)] = v.astype(BF)
        start(g3(c))

    def st4(c):
        landed(g3(c, True))
        start(g2(c))

    def st5(c):
        landed(g2(c, True))
        start(g1(c))

    def st6(c):
        landed(g1(c, True))
        off, size = chunks[c]
        for pos in range(4 * off, 4 * (off + size)):
            k = pos % 4
            tile = fin[k // 2, 2 * (k % 2):2 * (k % 2) + 2, :, pos // 4].reshape(ch, ch)
            if pos < 27:
                gw_ref[(pos % 3) * 9 + pos // 3] = tile
            else:
                gb_ref[...] = tile[0:16]

    st = [st0, st1, st2, st3, st4, st5, st6]
    acc[...] = jnp.zeros(acc.shape, F32)
    n = (nx + 2) // 2
    m = n // 2
    put(27, jnp.broadcast_to(gb, (ch, ch)))
    grad(0, 4, 0, n)
    tiles(0, 4)
    st[0](0)
    grad(4, 7, 0, m)
    st[1](0)
    grad(4, 7, m, n)
    tiles(4, 7)
    st[0](1)
    grad(7, 9, 0, m)
    st[2](0)
    st[1](1)
    grad(7, 9, m, n)
    tiles(7, 9)
    st[0](2)
    for s, c in ((3, 0), (2, 1), (1, 2), (4, 0), (3, 1), (5, 0), (2, 2), (4, 1), (6, 0), (5, 1), (3, 2),
                 (6, 1), (4, 2), (5, 2), (6, 2)):
        st[s](c)
    store.wait()
    for c in range(len(chunks)):
        for cs in (c1(c), c2(c), c3(c), c4(c), g3(c), g2(c), g1(c)):
            for r in cs:
                r.wait_send()


def local(nsx, nsy, volume, block_active, weight, bias, cotangent):
    _, nx, ny, nz, ch = volume.shape
    blocks = block_active.shape[3]
    rows = ny * nz
    chunks = ((0, 3), (3, 2), (5, 2))
    far = max(nsx // 2, 1)
    anyw = pl.BlockSpec(memory_space=pl.ANY)
    gr = (7, 16, ch)
    bf = lambda *dims: pltpu.VMEM(dims, BF)
    dma = pltpu.SemaphoreType.DMA
    out, gw, gb = pl.pallas_call(
        functools.partial(layer_kernel, nsx, nsy, nz // blocks, chunks),
        out_shape=(jax.ShapeDtypeStruct((nx, rows, ch), BF),
                   jax.ShapeDtypeStruct((27, ch, ch), BF),
                   jax.ShapeDtypeStruct((16, ch), BF)),
        in_specs=[SM, VM, anyw, anyw, anyw], out_specs=(anyw, VM, VM),
        scratch_shapes=[
            bf(2, ny, nz, ch), bf(2, nx, nz, ch), bf(2, ny, nz, ch), bf(2, nx + 2, nz, ch),
            bf(nx, ny, nz, ch), bf(36 * ch, 2 * ch), bf(nx, rows, ch), bf(nx, rows, ch),
            bf(nx + 2, rows + 2 * nz, 3 * ch), bf((nx + 4) * ch, rows), pltpu.VMEM((3 * ch, 9 * ch), F32),
            pltpu.VMEM((2, 16) + gr, F32), bf(16, *gr), bf(16, *gr), pltpu.VMEM((4, 4) + gr, F32),
            bf(4, 4, *gr), bf(4, 4, *gr), pltpu.VMEM((4,) + gr, F32), bf(4, *gr), bf(4, *gr),
            bf(far, *gr), bf(2, 4, 4, *gr), dma((9,)), dma((8,)), dma((8,)),
            dma((len(chunks), 13 + far)), dma((len(chunks), 13 + far))],
        compiler_params=pltpu.CompilerParams(collective_id=0, has_side_effects=True,
                                             vmem_limit_bytes=60 * 2**20),
        name="layer",
    )(block_active.reshape(blocks), jnp.concatenate([bias, bias])[None], volume[0],
      weight.reshape(27 * ch, ch), cotangent.reshape(nx, rows, ch))
    return (out.reshape(volume.shape), gw.reshape(weight.shape).astype(F32), gb[0].astype(F32))


def solution(mesh):
    tile = P("dp", "sx", "sy", None, None)
    return jax.shard_map(
        functools.partial(local, mesh.shape["sx"], mesh.shape["sy"]),
        mesh=mesh,
        in_specs=(tile, P("dp", "sx", "sy", None), P(), P(), tile),
        out_specs=(tile, P(), P()),
        check_vma=False,
    )
```

```python
import functools

import jax
import jax.numpy as jnp
from jax import lax
from jax.experimental import pallas as pl
from jax.experimental.pallas import tpu as pltpu
from jax.sharding import PartitionSpec as P

MESH = pl.DeviceIdType.MESH
VM = pl.BlockSpec(memory_space=pltpu.VMEM)
SM = pl.BlockSpec(memory_space=pltpu.SMEM)
NEAR = [(dx, dy) for dx in (-1, 0, 1) for dy in (-1, 0, 1) if (dx, dy) != (0, 0)]
BF = jnp.bfloat16
F32 = jnp.float32


def depth_mask(act_ref, rows, depth, edge):
    z = lax.rem(lax.broadcasted_iota(jnp.int32, (rows, 128), 0), depth)
    m = jnp.zeros((rows, 128), F32)
    for k in range(depth // edge):
        inside = jnp.logical_and(z >= k * edge, z < (k + 1) * edge)
        m = jnp.where(inside, act_ref[k].astype(F32), m)
    return m


def layer_kernel(nsx, nsy, edge, chunks, act_ref, bias_ref, vol_ref, w_ref, cot_ref,
                 out_ref, gw_ref, gb_ref, fx, fy, hx, hy, vb, wb, cb, ob, cols, dpt, acc, prea, preb,
                 g_ref, s1, r1, a1, s2, r2, a2, s3, r3, s4, fin, ls, hs, hr, ss, rs):
    nx, ny, nz, ch = vol_ref.shape
    rows = ny * nz
    d, x, y = lax.axis_index("dp"), lax.axis_index("sx"), lax.axis_index("sy")

    def there(dx, dy):
        return (x + dx >= 0) & (x + dx < nsx) & (y + dy >= 0) & (y + dy < nsy)

    h, dh = lax.rem(d, 2), d // 2
    xl, xh = lax.rem(x, 2), x // 2
    q = dh * 2 + xl
    far = nsx // 2

    def peer1():
        return {"dp": dh * 2 + 1 - h, "sx": x, "sy": y}

    def peer2(k):
        o = lax.rem(q + k, 4)
        return o, {"dp": (o // 2) * 2 + h, "sx": xh * 2 + lax.rem(o, 2), "sy": y}

    def peer3(k):
        o = lax.rem(y + k, 4)
        return o, {"dp": d, "sx": x, "sy": o}

    def peer4(k):
        o = lax.rem(xh + k, far)
        return o, {"dp": d, "sx": o * 2 + xl, "sy": y}

    peers = [peer1()] + [peer2(k)[1] for k in (1, 2, 3)] + [peer3(k)[1] for k in (1, 2, 3)]
    peers += [peer4(k)[1] for k in range(1, far)]
    barrier = pltpu.get_barrier_semaphore()
    for p in peers:
        pl.semaphore_signal(barrier, inc=1, device_id=p, device_id_type=MESH)
    for dx, dy in NEAR:
        @pl.when(there(dx, dy))
        def _():
            pl.semaphore_signal(barrier, inc=1, device_id={"sx": x + dx, "sy": y + dy},
                                device_id_type=MESH)
    load = [pltpu.make_async_copy(s, t, ls.at[k]) for k, (s, t) in enumerate((
        (vol_ref.at[0], fx.at[0]), (vol_ref.at[nx - 1], fx.at[1]),
        (vol_ref.at[:, 0], fy.at[0]), (vol_ref.at[:, ny - 1], fy.at[1]),
        (vol_ref, vb), (w_ref, wb.at[pl.ds(0, 27 * ch), pl.ds(0, ch)]),
        (w_ref, wb.at[pl.ds(9 * ch, 27 * ch), pl.ds(ch, ch)]), (cot_ref, cb)))]
    for r in load:
        r.start()
    zmask = depth_mask(act_ref, nz, nz, edge)[None].astype(BF)
    mask = depth_mask(act_ref, rows, nz, edge)
    wb[0:9 * ch, ch:2 * ch] = jnp.zeros((9 * ch, ch), BF)
    wb[27 * ch:36 * ch, 0:ch] = jnp.zeros((9 * ch, ch), BF)
    dpt[0:2 * ch, :] = jnp.zeros((2 * ch, rows), BF)
    dpt[(nx + 2) * ch:(nx + 4) * ch, :] = jnp.zeros((2 * ch, rows), BF)
    for r in load[:4]:
        r.wait()
    for side in range(2):
        fx[side] = fx[side] * zmask
        fy[side] = fy[side] * zmask
    pl.semaphore_wait(barrier, len(peers) + sum(there(dx, dy).astype(jnp.int32) for dx, dy in NEAR))

    def slot(dx, dy):
        if dy == 0:
            return hx.at[int(dx > 0)]
        if dx == 0:
            return hy.at[int(dy > 0), pl.ds(1, nx)]
        return hy.at[int(dy > 0), (nx + 1) * int(dx > 0)]

    def face(k):
        dx, dy = NEAR[k]
        if dy == 0:
            src = fx.at[int(dx > 0)]
        elif dx == 0:
            src = fy.at[int(dy > 0)]
        else:
            src = fx.at[int(dx > 0), (ny - 1) * int(dy > 0)]
        opp = NEAR.index((-dx, -dy))
        return pltpu.make_async_remote_copy(
            src_ref=src, dst_ref=slot(-dx, -dy), send_sem=hs.at[k], recv_sem=hr.at[opp],
            device_id={"sx": x + dx, "sy": y + dy}, device_id_type=MESH)

    for k, (dx, dy) in enumerate(NEAR):
        @pl.when(there(dx, dy))
        def _():
            face(k).start()

        @pl.when(jnp.logical_not(there(dx, dy)))
        def _():
            ref = slot(dx, dy)
            ref[...] = jnp.zeros(ref.shape, BF)

    z = lax.rem(lax.broadcasted_iota(jnp.int32, (rows, ch), 0), nz)
    first, last = z == 0, z == nz - 1

    def shifted(i, at, v):
        n = v.shape[0]
        here = pl.ds(at, n)
        cols[i, here, ch:2 * ch] = v.astype(BF)
        cols[i, here, 0:ch] = jnp.where(first[:n], 0.0, pltpu.roll(v, 1, 0)).astype(BF)
        cols[i, here, 2 * ch:3 * ch] = jnp.where(last[:n], 0.0, pltpu.roll(v, n - 1, 0)).astype(BF)

    load[4].wait()

    @pl.loop(0, nx)
    def _(i):
        shifted(i + 1, nz, vb[i].reshape(rows, ch).astype(F32) * mask)

    for k, (dx, dy) in enumerate(NEAR):
        @pl.when(there(dx, dy))
        def _():
            face(k).wait_send()
            face(NEAR.index((-dx, -dy))).wait_recv()
    for side in range(2):
        shifted(side * (nx + 1), nz, hx[side].reshape(rows, ch).astype(F32))

    @pl.loop(0, nx + 2)
    def _(i):
        for side in range(2):
            shifted(i, side * (nz + rows), hy[side, i].astype(F32))

    for r in load[5:]:
        r.wait()
    half = 18 * ch

    bias2 = jnp.concatenate([bias_ref[...], bias_ref[...]], axis=1)

    def conv(p, into):
        pre = jnp.zeros((rows, 2 * ch), F32) + bias2
        for j in range(2):
            lhs = jnp.concatenate(
                [cols[2 * p + 2 * j + t, pl.ds(b * nz, rows), :] for t in range(2) for b in range(3)], axis=1)
            pre = pre + jnp.dot(lhs, wb[j * half:(j + 1) * half, :], preferred_element_type=F32)
        into[...] = pre

    def finish(p, pre, gb):
        for t in range(2):
            u = pre[:, t * ch:(t + 1) * ch]
            sig = jax.nn.sigmoid(u)
            ob[2 * p + t] = (u * sig * mask).astype(BF)
            e = (cb[2 * p + t].astype(F32) * sig * (1.0 + u * (1.0 - sig)) * mask).astype(BF)
            gb = gb + jnp.sum(e.astype(F32), axis=0, keepdims=True)
            at = (2 * p + t + 2) * ch
            dpt[pl.ds(at if isinstance(at, int) else pl.multiple_of(at, ch), ch), :] = e.T
        return gb

    def pairs(k, gb):
        conv(2 * k + 1, preb)
        gb = finish(2 * k, prea, gb)
        conv(2 * k + 2, prea)
        return finish(2 * k + 1, preb, gb)

    conv(0, prea)
    gb = lax.fori_loop(0, nx // 4 - 1, pairs, jnp.zeros((1, ch), F32))
    conv(nx // 2 - 1, preb)
    gb = finish(nx // 2 - 2, prea, gb)
    gb = finish(nx // 2 - 1, preb, gb)
    store = pltpu.make_async_copy(ob, out_ref, ls.at[8])
    store.start()

    def grad(q0, q1, i0, i1):
        @pl.loop(i0, i1)
        def _(p):
            i = 2 * p
            lhs = jnp.concatenate(
                [dpt[pl.ds(pl.multiple_of((i + t) * ch, ch), 3 * ch), :] for t in range(2)], axis=1)
            rhs = jnp.concatenate([jnp.concatenate(
                [cols[i + t, pl.ds((o // 3) * nz, rows), (o % 3) * ch:(o % 3 + 1) * ch] for o in range(q0, q1)],
                axis=1) for t in range(2)], axis=0)
            acc[:, q0 * ch:q1 * ch] += jnp.dot(lhs, rhs, preferred_element_type=F32)

    def put(pos, tile):
        g_ref[pos % 4 // 2, pl.ds(8 * (pos % 2), 8), pos // 4] = tile.reshape(8, 16, ch)

    def tiles(q0, q1):
        for o in range(q0, q1):
            for a in range(3):
                put(o * 3 + a, acc[(2 - a) * ch:(3 - a) * ch, o * ch:(o + 1) * ch].T)

    def rcopy(src, dst, c, n, p):
        return pltpu.make_async_remote_copy(src_ref=src, dst_ref=dst, send_sem=ss.at[c, n],
                                            recv_sem=rs.at[c, n], device_id=p, device_id_type=MESH)

    def part(c):
        off, size = chunks[c]
        return pl.ds(off, size)

    def c1(c):
        return [rcopy(s1.at[:, part(c)], r1.at[:, part(c)], c, 0, peer1())]

    def c2(c):
        cs = []
        for k in (1, 2, 3):
            o, p = peer2(k)
            cs.append(rcopy(s2.at[o, :, part(c)], r2.at[k, :, part(c)], c, k, p))
        return cs

    def c3(c):
        cs = []
        for k in (1, 2, 3):
            o, p = peer3(k)
            cs.append(rcopy(s3.at[o, part(c)], r3.at[k, part(c)], c, 3 + k, p))
        return cs

    def c4(c):
        cs = []
        for k in range(1, far):
            o, p = peer4(k)
            cs.append(rcopy(s4.at[xh, part(c)], s4.at[xh, part(c)], c, 13 + k, p))
        return cs

    def c4in(c):
        cs = []
        for k in range(1, far):
            o, p = peer4(far - k)
            cs.append(rcopy(s4.at[xh, part(c)], s4.at[o, part(c)], c, 13 + k, p))
        return cs

    def g3(c, inn=False):
        cs = []
        for k in (1, 2, 3):
            o, p = peer3(4 - k if inn else k)
            cs.append(rcopy(fin.at[h, q, y, part(c)], fin.at[h, q, o if inn else y, part(c)], c, 6 + k, p))
        return cs

    def g2(c, inn=False):
        cs = []
        for k in (1, 2, 3):
            o, p = peer2(4 - k if inn else k)
            cs.append(rcopy(fin.at[h, q, :, part(c)], fin.at[h, o if inn else q, :, part(c)], c, 9 + k, p))
        return cs

    def g1(c, inn=False):
        return [rcopy(fin.at[h, :, :, part(c)], fin.at[1 - h if inn else h, :, :, part(c)], c, 13, peer1())]

    def start(cs):
        for r in cs:
            r.start()

    def landed(cs):
        for r in cs:
            r.wait_recv()

    def st0(c):
        s1[:, part(c)] = g_ref[1 - h, :, part(c)].astype(BF)
        start(c1(c))

    def st1(c):
        landed(c1(c))
        v = g_ref[h, :, part(c)] + r1[:, part(c)].astype(F32)
        v = v.reshape((4, 4) + v.shape[1:])
        a1[:, :, part(c)] = v
        s2[:, :, part(c)] = v.astype(BF)
        start(c2(c))

    def st2(c):
        landed(c2(c))
        v = a1[q, :, part(c)]
        for k in (1, 2, 3):
            v = v + r2[k, :, part(c)].astype(F32)
        a2[:, part(c)] = v
        s3[:, part(c)] = v.astype(BF)
        start(c3(c))

    def st3(c):
        landed(c3(c))
        v = a2[y, part(c)]
        for k in (1, 2, 3):
            v = v + r3[k, part(c)].astype(F32)
        if far > 1:
            s4[xh, part(c)] = v.astype(BF)
            start(c4(c))
            landed(c4in(c))
            v = s4[0, part(c)].astype(F32)
            for k in range(1, far):
                v = v + s4[k, part(c)].astype(F32)
        fin[h, q, y, part(c)] = v.astype(BF)
        start(g3(c))

    def st4(c):
        landed(g3(c, True))
        start(g2(c))

    def st5(c):
        landed(g2(c, True))
        start(g1(c))

    def st6(c):
        landed(g1(c, True))
        off, size = chunks[c]
        for pos in range(4 * off, 4 * (off + size)):
            k = pos % 4
            tile = fin[k // 2, 2 * (k % 2):2 * (k % 2) + 2, :, pos // 4].reshape(ch, ch)
            if pos < 27:
                gw_ref[(pos % 3) * 9 + pos // 3] = tile.astype(F32)
            else:
                gb_ref[...] = tile[0:16].astype(F32)[0:1]

    st = [st0, st1, st2, st3, st4, st5, st6]
    acc[...] = jnp.zeros(acc.shape, F32)
    n = (nx + 2) // 2
    put(27, jnp.broadcast_to(gb, (ch, ch)))
    ready = {0: (0,), 1: (1, 2), 2: (3,), 3: (4, 5), 4: (6,)}
    at = {}
    step = 0
    while step < 5 or any(v < 7 for v in at.values()):
        if step < 5:
            q0, q1 = 2 * step, min(2 * step + 2, 9)
            grad(q0, q1, 0, n)
            tiles(q0, q1)
        for c in sorted(at):
            if at[c] < 7:
                st[at[c]](c)
                at[c] += 1
        for c in ready.get(step, ()):
            st[0](c)
            at[c] = 1
        step += 1
    store.wait()
    for c in range(len(chunks)):
        for cs in (c1(c), c2(c), c3(c), c4(c), g3(c), g2(c), g1(c)):
            for r in cs:
                r.wait_send()


def local(nsx, nsy, volume, block_active, weight, bias, cotangent):
    _, nx, ny, nz, ch = volume.shape
    blocks = block_active.shape[3]
    rows = ny * nz
    chunks = tuple((k, 1) for k in range(7))
    far = max(nsx // 2, 1)
    anyw = pl.BlockSpec(memory_space=pl.ANY)
    gr = (7, 16, ch)
    bf = lambda *dims: pltpu.VMEM(dims, BF)
    dma = pltpu.SemaphoreType.DMA
    out, gw, gb = pl.pallas_call(
        functools.partial(layer_kernel, nsx, nsy, nz // blocks, chunks),
        out_shape=(jax.ShapeDtypeStruct((nx, rows, ch), BF),
                   jax.ShapeDtypeStruct((27, ch, ch), F32),
                   jax.ShapeDtypeStruct((1, ch), F32)),
        in_specs=[SM, VM, anyw, anyw, anyw], out_specs=(anyw, VM, VM),
        scratch_shapes=[
            bf(2, ny, nz, ch), bf(2, nx, nz, ch), bf(2, ny, nz, ch), bf(2, nx + 2, nz, ch),
            bf(nx, ny, nz, ch), bf(36 * ch, 2 * ch), bf(nx, rows, ch), bf(nx, rows, ch),
            bf(nx + 2, rows + 2 * nz, 3 * ch), bf((nx + 4) * ch, rows), pltpu.VMEM((3 * ch, 9 * ch), F32),
            pltpu.VMEM((rows, 2 * ch), F32), pltpu.VMEM((rows, 2 * ch), F32),
            pltpu.VMEM((2, 16) + gr, F32), bf(16, *gr), bf(16, *gr), pltpu.VMEM((4, 4) + gr, F32),
            bf(4, 4, *gr), bf(4, 4, *gr), pltpu.VMEM((4,) + gr, F32), bf(4, *gr), bf(4, *gr),
            bf(far, *gr), bf(2, 4, 4, *gr), dma((9,)), dma((8,)), dma((8,)),
            dma((len(chunks), 13 + far)), dma((len(chunks), 13 + far))],
        compiler_params=pltpu.CompilerParams(collective_id=0, has_side_effects=True,
                                             vmem_limit_bytes=60 * 2**20),
        name="layer",
    )(block_active.reshape(blocks), bias[None], volume[0],
      weight.reshape(27 * ch, ch), cotangent.reshape(nx, rows, ch))
    return (out.reshape(volume.shape), gw.reshape(weight.shape), gb.reshape(ch))


def solution(mesh):
    tile = P("dp", "sx", "sy", None, None)
    return jax.shard_map(
        functools.partial(local, mesh.shape["sx"], mesh.shape["sy"]),
        mesh=mesh,
        in_specs=(tile, P("dp", "sx", "sy", None), P(), P(), tile),
        out_specs=(tile, P(), P()),
        check_vma=False,
    )
```

```python
import functools

import jax
import jax.numpy as jnp
from jax import lax
from jax.experimental import pallas as pl
from jax.experimental.pallas import tpu as pltpu
from jax.sharding import PartitionSpec as P

MESH = pl.DeviceIdType.MESH
VM = pl.BlockSpec(memory_space=pltpu.VMEM)
SM = pl.BlockSpec(memory_space=pltpu.SMEM)
NEAR = [(dx, dy) for dx in (-1, 0, 1) for dy in (-1, 0, 1) if (dx, dy) != (0, 0)]
BF = jnp.bfloat16
F32 = jnp.float32


def depth_mask(act_ref, rows, depth, edge):
    z = lax.rem(lax.broadcasted_iota(jnp.int32, (rows, 128), 0), depth)
    m = jnp.zeros((rows, 128), F32)
    for k in range(depth // edge):
        inside = jnp.logical_and(z >= k * edge, z < (k + 1) * edge)
        m = jnp.where(inside, act_ref[k].astype(F32), m)
    return m


def layer_kernel(nsx, nsy, edge, chunks, act_ref, bias_ref, vol_ref, w_ref, cot_ref,
                 out_ref, gw_ref, fx, fy, hx, hy, vb, wb, cb, ob, cols, dpt, acc, prea, preb,
                 g_ref, s1, r1, a1, s2, r2, a2, s3, r3, s4, s8, r8, fin, ls, hs, hr, ss, rs):
    nx, ny, nz, ch = vol_ref.shape
    rows = ny * nz
    d, x, y = lax.axis_index("dp"), lax.axis_index("sx"), lax.axis_index("sy")

    def there(dx, dy):
        return (x + dx >= 0) & (x + dx < nsx) & (y + dy >= 0) & (y + dy < nsy)

    h, dh = lax.rem(d, 2), d // 2
    xl, xh = lax.rem(x, 2), x // 2
    q = dh * 2 + xl
    far = nsx // 2

    def peer1():
        return {"dp": dh * 2 + 1 - h, "sx": x, "sy": y}

    def peer2(k):
        o = lax.rem(q + k, 4)
        return o, {"dp": (o // 2) * 2 + h, "sx": xh * 2 + lax.rem(o, 2), "sy": y}

    def peer3(k):
        o = lax.rem(y + k, 4)
        return o, {"dp": d, "sx": x, "sy": o}

    def peer4(k):
        o = lax.rem(xh + k, far)
        return o, {"dp": d, "sx": o * 2 + xl, "sy": y}

    def peer8(k):
        o = lax.rem(h * 4 + q + k, 8)
        oq = lax.rem(o, 4)
        return o // 4, oq, {"dp": (oq // 2) * 2 + o // 4, "sx": xh * 2 + lax.rem(oq, 2), "sy": y}

    peers = [peer8(k)[2] for k in range(1, 8)] + [peer3(k)[1] for k in (1, 2, 3)]
    peers += [peer4(k)[1] for k in range(1, far)]
    barrier = pltpu.get_barrier_semaphore()
    for p in peers:
        pl.semaphore_signal(barrier, inc=1, device_id=p, device_id_type=MESH)
    for dx, dy in NEAR:
        @pl.when(there(dx, dy))
        def _():
            pl.semaphore_signal(barrier, inc=1, device_id={"sx": x + dx, "sy": y + dy},
                                device_id_type=MESH)
    load = [pltpu.make_async_copy(s, t, ls.at[k]) for k, (s, t) in enumerate((
        (vol_ref.at[0], fx.at[0]), (vol_ref.at[nx - 1], fx.at[1]),
        (vol_ref.at[:, 0], fy.at[0]), (vol_ref.at[:, ny - 1], fy.at[1]),
        (vol_ref, vb), (w_ref, wb.at[pl.ds(0, 27 * ch), pl.ds(0, ch)]),
        (w_ref, wb.at[pl.ds(9 * ch, 27 * ch), pl.ds(ch, ch)]), (cot_ref, cb)))]
    for r in load:
        r.start()
    zmask = depth_mask(act_ref, nz, nz, edge)[None].astype(BF)
    mask = depth_mask(act_ref, rows, nz, edge)
    wb[0:9 * ch, ch:2 * ch] = jnp.zeros((9 * ch, ch), BF)
    wb[27 * ch:36 * ch, 0:ch] = jnp.zeros((9 * ch, ch), BF)
    dpt[0:2 * ch, :] = jnp.zeros((2 * ch, rows), BF)
    dpt[(nx + 2) * ch:(nx + 4) * ch, :] = jnp.zeros((2 * ch, rows), BF)
    for r in load[:4]:
        r.wait()
    for side in range(2):
        fx[side] = fx[side] * zmask
        fy[side] = fy[side] * zmask
    pl.semaphore_wait(barrier, len(peers) + sum(there(dx, dy).astype(jnp.int32) for dx, dy in NEAR))

    def slot(dx, dy):
        if dy == 0:
            return hx.at[int(dx > 0)]
        if dx == 0:
            return hy.at[int(dy > 0), pl.ds(1, nx)]
        return hy.at[int(dy > 0), (nx + 1) * int(dx > 0)]

    def face(k):
        dx, dy = NEAR[k]
        if dy == 0:
            src = fx.at[int(dx > 0)]
        elif dx == 0:
            src = fy.at[int(dy > 0)]
        else:
            src = fx.at[int(dx > 0), (ny - 1) * int(dy > 0)]
        opp = NEAR.index((-dx, -dy))
        return pltpu.make_async_remote_copy(
            src_ref=src, dst_ref=slot(-dx, -dy), send_sem=hs.at[k], recv_sem=hr.at[opp],
            device_id={"sx": x + dx, "sy": y + dy}, device_id_type=MESH)

    for k, (dx, dy) in enumerate(NEAR):
        @pl.when(there(dx, dy))
        def _():
            face(k).start()

        @pl.when(jnp.logical_not(there(dx, dy)))
        def _():
            ref = slot(dx, dy)
            ref[...] = jnp.zeros(ref.shape, BF)

    z = lax.rem(lax.broadcasted_iota(jnp.int32, (rows, ch), 0), nz)
    first, last = z == 0, z == nz - 1

    def shifted(i, at, v):
        n = v.shape[0]
        here = pl.ds(at, n)
        cols[i, here, ch:2 * ch] = v.astype(BF)
        cols[i, here, 0:ch] = jnp.where(first[:n], 0.0, pltpu.roll(v, 1, 0)).astype(BF)
        cols[i, here, 2 * ch:3 * ch] = jnp.where(last[:n], 0.0, pltpu.roll(v, n - 1, 0)).astype(BF)

    load[4].wait()

    @pl.loop(0, nx)
    def _(i):
        shifted(i + 1, nz, vb[i].reshape(rows, ch).astype(F32) * mask)

    for k, (dx, dy) in enumerate(NEAR):
        @pl.when(there(dx, dy))
        def _():
            face(k).wait_send()
            face(NEAR.index((-dx, -dy))).wait_recv()
    for side in range(2):
        shifted(side * (nx + 1), nz, hx[side].reshape(rows, ch).astype(F32))

    @pl.loop(0, nx + 2)
    def _(i):
        for side in range(2):
            shifted(i, side * (nz + rows), hy[side, i].astype(F32))

    for r in load[5:]:
        r.wait()
    half = 18 * ch

    bias2 = jnp.concatenate([bias_ref[...], bias_ref[...]], axis=1)

    def conv(p, into):
        pre = jnp.zeros((rows, 2 * ch), F32) + bias2
        for j in range(2):
            lhs = jnp.concatenate(
                [cols[2 * p + 2 * j + t, pl.ds(b * nz, rows), :] for t in range(2) for b in range(3)], axis=1)
            pre = pre + jnp.dot(lhs, wb[j * half:(j + 1) * half, :], preferred_element_type=F32)
        into[...] = pre

    def finish(p, pre, gb):
        for t in range(2):
            u = pre[:, t * ch:(t + 1) * ch]
            sig = jax.nn.sigmoid(u)
            ob[2 * p + t] = (u * sig * mask).astype(BF)
            e = (cb[2 * p + t].astype(F32) * sig * (1.0 + u * (1.0 - sig)) * mask).astype(BF)
            gb = gb + jnp.sum(e.astype(F32), axis=0, keepdims=True)
            at = (2 * p + t + 2) * ch
            dpt[pl.ds(at if isinstance(at, int) else pl.multiple_of(at, ch), ch), :] = e.T
        return gb

    def pairs(k, gb):
        conv(2 * k + 1, preb)
        gb = finish(2 * k, prea, gb)
        conv(2 * k + 2, prea)
        return finish(2 * k + 1, preb, gb)

    conv(0, prea)
    gb = lax.fori_loop(0, nx // 4 - 1, pairs, jnp.zeros((1, ch), F32))
    conv(nx // 2 - 1, preb)
    gb = finish(nx // 2 - 2, prea, gb)
    gb = finish(nx // 2 - 1, preb, gb)
    store = pltpu.make_async_copy(ob, out_ref, ls.at[8])
    store.start()

    def grad(q0, q1, i0, i1):
        @pl.loop(i0, i1)
        def _(p):
            i = 2 * p
            lhs = jnp.concatenate(
                [dpt[pl.ds(pl.multiple_of((i + t) * ch, ch), 3 * ch), :] for t in range(2)], axis=1)
            rhs = jnp.concatenate([jnp.concatenate(
                [cols[i + t, pl.ds((o // 3) * nz, rows), (o % 3) * ch:(o % 3 + 1) * ch] for o in range(q0, q1)],
                axis=1) for t in range(2)], axis=0)
            acc[:, q0 * ch:q1 * ch] += jnp.dot(lhs, rhs, preferred_element_type=F32)

    def put(pos, tile):
        g_ref[pos // 4, pos % 4 // 2, pl.ds(2 * (pos % 2), 2)] = tile.reshape(2, 4, 16, ch)

    def tiles(q0, q1):
        for o in range(q0, q1):
            for a in range(3):
                put(o * 3 + a, acc[(2 - a) * ch:(3 - a) * ch, o * ch:(o + 1) * ch].T)

    def rcopy(src, dst, c, n, p):
        return pltpu.make_async_remote_copy(src_ref=src, dst_ref=dst, send_sem=ss.at[c, n],
                                            recv_sem=rs.at[c, n], device_id=p, device_id_type=MESH)

    def part(c):
        off, size = chunks[c]
        return pl.ds(off, size)

    def c1(c):
        return [rcopy(s1.at[part(c)], r1.at[part(c)], c, 0, peer1())]

    def c2(c):
        return [rcopy(s2.at[part(c), o], r2.at[part(c), k], c, k, p)
                for k in (1, 2, 3) for o, p in [peer2(k)]]

    def c3(c):
        return [rcopy(s3.at[part(c), o], r3.at[part(c), k], c, 3 + k, p)
                for k in (1, 2, 3) for o, p in [peer3(k)]]

    def c4(c):
        return [rcopy(s4.at[part(c), xh], s4.at[part(c), xh], c, 27 + k, p)
                for k in range(1, far) for o, p in [peer4(k)]]

    def c4in(c):
        return [rcopy(s4.at[part(c), xh], s4.at[part(c), o], c, 27 + k, p)
                for k in range(1, far) for o, p in [peer4(far - k)]]

    def c8(c):
        return [rcopy(s8.at[part(c), oh, oq], r8.at[part(c), k], c, 13 + k, p)
                for k in range(1, 8) for oh, oq, p in [peer8(k)]]

    def g3(c, inn=False):
        return [rcopy(fin.at[part(c), h, q, y], fin.at[part(c), h, q, o if inn else y], c, 6 + k, p)
                for k in (1, 2, 3) for o, p in [peer3(4 - k if inn else k)]]

    def g2(c, inn=False):
        return [rcopy(fin.at[part(c), h, q], fin.at[part(c), h, o if inn else q], c, 9 + k, p)
                for k in (1, 2, 3) for o, p in [peer2(4 - k if inn else k)]]

    def g1(c, inn=False):
        return [rcopy(fin.at[part(c), h], fin.at[part(c), 1 - h if inn else h], c, 13, peer1())]

    def g8(c, inn=False):
        return [rcopy(fin.at[part(c), h, q], fin.at[part(c), oh if inn else h, oq if inn else q],
                      c, 20 + k, p)
                for k in range(1, 8) for oh, oq, p in [peer8(8 - k if inn else k)]]

    def start(cs):
        for r in cs:
            r.start()

    def landed(cs):
        for r in cs:
            r.wait_recv()

    def st0(c):
        s1[part(c)] = g_ref[part(c), 1 - h].astype(BF)
        start(c1(c))

    def st1(c):
        landed(c1(c))
        v = g_ref[part(c), h] + r1[part(c)].astype(F32)
        a1[part(c)] = v
        s2[part(c)] = v.astype(BF)
        start(c2(c))

    def onward(c, v):
        a2[part(c)] = v
        s3[part(c)] = v.astype(BF)
        start(c3(c))

    def st2(c):
        landed(c2(c))
        v = a1[part(c), q]
        for k in (1, 2, 3):
            v = v + r2[part(c), k].astype(F32)
        onward(c, v)

    def w0(c):
        s8[part(c)] = g_ref[part(c)].astype(BF)
        start(c8(c))

    def w1(c):
        landed(c8(c))
        v = g_ref[part(c), h, q]
        for k in range(1, 8):
            v = v + r8[part(c), k].astype(F32)
        onward(c, v)

    def st3(c):
        landed(c3(c))
        v = a2[part(c), y]
        for k in (1, 2, 3):
            v = v + r3[part(c), k].astype(F32)
        if far > 1:
            s4[part(c), xh] = v.astype(BF)
            start(c4(c))
            landed(c4in(c))
            v = s4[part(c), 0].astype(F32)
            for k in range(1, far):
                v = v + s4[part(c), k].astype(F32)
        fin[part(c), h, q, y] = v.astype(BF)
        start(g3(c))

    def st4(c):
        landed(g3(c, True))
        start(g2(c))

    def st5(c):
        landed(g2(c, True))
        start(g1(c))

    def result(c):
        off, size = chunks[c]
        for pos in range(4 * off, 4 * (off + size)):
            k = pos % 4
            tile = fin[pos // 4, k // 2, 2 * (k % 2):2 * (k % 2) + 2].reshape(ch, ch)
            gw_ref[(pos % 3) * 9 + pos // 3 if pos < 27 else 27] = tile.astype(F32)

    def st6(c):
        landed(g1(c, True))
        result(c)

    def w3(c):
        landed(g3(c, True))
        start(g8(c))

    def w4(c):
        landed(g8(c, True))
        result(c)

    far_way = [st0, st1, st2, st3, st4, st5, st6]
    short_way = [w0, w1, st3, w3, w4]
    way = [far_way, far_way, short_way, short_way]
    acc[...] = jnp.zeros(acc.shape, F32)
    n = (nx + 2) // 2
    put(27, jnp.broadcast_to(gb, (ch, ch)))
    ready = {1: (0,), 2: (1,), 3: (2,), 4: (3,)}
    at = {}
    step = 0
    while step < 5 or any(v < len(way[c]) for c, v in at.items()):
        if step < 5:
            q0, q1 = 2 * step, min(2 * step + 2, 9)
            grad(q0, q1, 0, n)
            tiles(q0, q1)
        for c in sorted(at):
            if at[c] < len(way[c]):
                way[c][at[c]](c)
                at[c] += 1
        for c in ready.get(step, ()):
            way[c][0](c)
            at[c] = 1
        step += 1
    store.wait()
    for c in range(len(chunks)):
        long = way[c] is far_way
        for cs in (c3(c), c4(c), g3(c)) + ((c1(c), c2(c), g2(c), g1(c)) if long else (c8(c), g8(c))):
            for r in cs:
                r.wait_send()


def local(nsx, nsy, volume, block_active, weight, bias, cotangent):
    _, nx, ny, nz, ch = volume.shape
    blocks = block_active.shape[3]
    rows = ny * nz
    chunks = ((0, 3), (3, 1), (4, 2), (6, 1))
    far = max(nsx // 2, 1)
    anyw = pl.BlockSpec(memory_space=pl.ANY)
    gr = (16, ch)
    bf = lambda *dims: pltpu.VMEM(dims, BF)
    dma = pltpu.SemaphoreType.DMA
    out, gw = pl.pallas_call(
        functools.partial(layer_kernel, nsx, nsy, nz // blocks, chunks),
        out_shape=(jax.ShapeDtypeStruct((nx, rows, ch), BF),
                   jax.ShapeDtypeStruct((28, ch, ch), F32)),
        in_specs=[SM, VM, anyw, anyw, anyw], out_specs=(anyw, VM),
        scratch_shapes=[
            bf(2, ny, nz, ch), bf(2, nx, nz, ch), bf(2, ny, nz, ch), bf(2, nx + 2, nz, ch),
            bf(nx, ny, nz, ch), bf(36 * ch, 2 * ch), bf(nx, rows, ch), bf(nx, rows, ch),
            bf(nx + 2, rows + 2 * nz, 3 * ch), bf((nx + 4) * ch, rows), pltpu.VMEM((3 * ch, 9 * ch), F32),
            pltpu.VMEM((rows, 2 * ch), F32), pltpu.VMEM((rows, 2 * ch), F32),
            pltpu.VMEM((7, 2, 4, 4) + gr, F32), bf(7, 4, 4, *gr), bf(7, 4, 4, *gr),
            pltpu.VMEM((7, 4, 4) + gr, F32), bf(7, 4, 4, *gr), bf(7, 4, 4, *gr),
            pltpu.VMEM((7, 4) + gr, F32), bf(7, 4, *gr), bf(7, 4, *gr), bf(7, far, *gr),
            bf(7, 2, 4, 4, *gr), bf(7, 8, 4, *gr), bf(7, 2, 4, 4, *gr), dma((9,)), dma((8,)), dma((8,)),
            dma((len(chunks), 27 + far)), dma((len(chunks), 27 + far))],
        compiler_params=pltpu.CompilerParams(collective_id=0, has_side_effects=True,
                                             vmem_limit_bytes=60 * 2**20),
        name="layer",
    )(block_active.reshape(blocks), bias[None], volume[0],
      weight.reshape(27 * ch, ch), cotangent.reshape(nx, rows, ch))
    return (out.reshape(volume.shape), gw[:27].reshape(weight.shape), gw[27, 0])


def solution(mesh):
    tile = P("dp", "sx", "sy", None, None)
    return jax.shard_map(
        functools.partial(local, mesh.shape["sx"], mesh.shape["sy"]),
        mesh=mesh,
        in_specs=(tile, P("dp", "sx", "sy", None), P(), P(), tile),
        out_specs=(tile, P(), P()),
        check_vma=False,
    )
```

```python
import functools

import jax
import jax.numpy as jnp
from jax import lax
from jax.experimental import pallas as pl
from jax.experimental.pallas import tpu as pltpu
from jax.sharding import PartitionSpec as P

MESH = pl.DeviceIdType.MESH
VM = pl.BlockSpec(memory_space=pltpu.VMEM)
SM = pl.BlockSpec(memory_space=pltpu.SMEM)
NEAR = [(dx, dy) for dx in (-1, 0, 1) for dy in (-1, 0, 1) if (dx, dy) != (0, 0)]
BF = jnp.bfloat16
F32 = jnp.float32


def depth_mask(act_ref, rows, depth, edge):
    z = lax.rem(lax.broadcasted_iota(jnp.int32, (rows, 128), 0), depth)
    m = jnp.zeros((rows, 128), F32)
    for k in range(depth // edge):
        inside = jnp.logical_and(z >= k * edge, z < (k + 1) * edge)
        m = jnp.where(inside, act_ref[k].astype(F32), m)
    return m


def layer_kernel(nsx, nsy, edge, chunks, act_ref, bias_ref, vol_ref, w_ref, cot_ref,
                 out_ref, gw_ref, fx, fy, hx, hy, vb, wb, cb, ob, cols, dpt, acc, prea, preb,
                 g_ref, s1, r1, a1, s2, r2, a2, s3, r3, s4, s8, r8, fin, ls, hs, hr, ss, rs):
    nx, ny, nz, ch = vol_ref.shape
    rows = ny * nz
    d, x, y = lax.axis_index("dp"), lax.axis_index("sx"), lax.axis_index("sy")

    def there(dx, dy):
        return (x + dx >= 0) & (x + dx < nsx) & (y + dy >= 0) & (y + dy < nsy)

    h, dh = lax.rem(d, 2), d // 2
    xl, xh = lax.rem(x, 2), x // 2
    q = dh * 2 + xl
    far = nsx // 2

    def peer1():
        return {"dp": dh * 2 + 1 - h, "sx": x, "sy": y}

    def peer2(k):
        o = lax.rem(q + k, 4)
        return o, {"dp": (o // 2) * 2 + h, "sx": xh * 2 + lax.rem(o, 2), "sy": y}

    def peer3(k):
        o = lax.rem(y + k, 4)
        return o, {"dp": d, "sx": x, "sy": o}

    def peer4(k):
        o = lax.rem(xh + k, far)
        return o, {"dp": d, "sx": o * 2 + xl, "sy": y}

    def peer8(k):
        o = lax.rem(h * 4 + q + k, 8)
        oq = lax.rem(o, 4)
        return o // 4, oq, {"dp": (oq // 2) * 2 + o // 4, "sx": xh * 2 + lax.rem(oq, 2), "sy": y}

    peers = [peer8(k)[2] for k in range(1, 8)] + [peer3(k)[1] for k in (1, 2, 3)]
    peers += [peer4(k)[1] for k in range(1, far)]
    barrier = pltpu.get_barrier_semaphore()
    for p in peers:
        pl.semaphore_signal(barrier, inc=1, device_id=p, device_id_type=MESH)
    for dx, dy in NEAR:
        @pl.when(there(dx, dy))
        def _():
            pl.semaphore_signal(barrier, inc=1, device_id={"sx": x + dx, "sy": y + dy},
                                device_id_type=MESH)
    load = [pltpu.make_async_copy(s, t, ls.at[k]) for k, (s, t) in enumerate((
        (vol_ref.at[0], fx.at[0]), (vol_ref.at[nx - 1], fx.at[1]),
        (vol_ref.at[:, 0], fy.at[0]), (vol_ref.at[:, ny - 1], fy.at[1]),
        (vol_ref, vb), (w_ref, wb.at[pl.ds(0, 27 * ch), pl.ds(0, ch)]),
        (w_ref, wb.at[pl.ds(9 * ch, 27 * ch), pl.ds(ch, ch)]), (cot_ref, cb)))]
    for r in load:
        r.start()
    zmask = depth_mask(act_ref, nz, nz, edge)[None].astype(BF)
    mask = depth_mask(act_ref, rows, nz, edge)
    wb[0:9 * ch, ch:2 * ch] = jnp.zeros((9 * ch, ch), BF)
    wb[27 * ch:36 * ch, 0:ch] = jnp.zeros((9 * ch, ch), BF)
    dpt[0:2 * ch, :] = jnp.zeros((2 * ch, rows), BF)
    dpt[(nx + 2) * ch:(nx + 4) * ch, :] = jnp.zeros((2 * ch, rows), BF)
    for r in load[:4]:
        r.wait()
    for side in range(2):
        fx[side] = fx[side] * zmask
        fy[side] = fy[side] * zmask
    pl.semaphore_wait(barrier, len(peers) + sum(there(dx, dy).astype(jnp.int32) for dx, dy in NEAR))

    def slot(dx, dy):
        if dy == 0:
            return hx.at[int(dx > 0)]
        if dx == 0:
            return hy.at[int(dy > 0), pl.ds(1, nx)]
        return hy.at[int(dy > 0), (nx + 1) * int(dx > 0)]

    def face(k):
        dx, dy = NEAR[k]
        if dy == 0:
            src = fx.at[int(dx > 0)]
        elif dx == 0:
            src = fy.at[int(dy > 0)]
        else:
            src = fx.at[int(dx > 0), (ny - 1) * int(dy > 0)]
        opp = NEAR.index((-dx, -dy))
        return pltpu.make_async_remote_copy(
            src_ref=src, dst_ref=slot(-dx, -dy), send_sem=hs.at[k], recv_sem=hr.at[opp],
            device_id={"sx": x + dx, "sy": y + dy}, device_id_type=MESH)

    for k, (dx, dy) in enumerate(NEAR):
        @pl.when(there(dx, dy))
        def _():
            face(k).start()

        @pl.when(jnp.logical_not(there(dx, dy)))
        def _():
            ref = slot(dx, dy)
            ref[...] = jnp.zeros(ref.shape, BF)

    z = lax.rem(lax.broadcasted_iota(jnp.int32, (rows, ch), 0), nz)
    first, last = z == 0, z == nz - 1

    def shifted(i, at, v):
        n = v.shape[0]
        here = pl.ds(at, n)
        cols[i, here, ch:2 * ch] = v.astype(BF)
        cols[i, here, 0:ch] = jnp.where(first[:n], 0.0, pltpu.roll(v, 1, 0)).astype(BF)
        cols[i, here, 2 * ch:3 * ch] = jnp.where(last[:n], 0.0, pltpu.roll(v, n - 1, 0)).astype(BF)

    load[4].wait()

    @pl.loop(0, nx)
    def _(i):
        shifted(i + 1, nz, vb[i].reshape(rows, ch).astype(F32) * mask)

    for k, (dx, dy) in enumerate(NEAR):
        @pl.when(there(dx, dy))
        def _():
            face(k).wait_send()
            face(NEAR.index((-dx, -dy))).wait_recv()
    for side in range(2):
        shifted(side * (nx + 1), nz, hx[side].reshape(rows, ch).astype(F32))

    @pl.loop(0, nx + 2)
    def _(i):
        for side in range(2):
            shifted(i, side * (nz + rows), hy[side, i].astype(F32))

    for r in load[5:]:
        r.wait()
    half = 18 * ch

    bias2 = jnp.concatenate([bias_ref[...], bias_ref[...]], axis=1)

    def conv(p, into):
        pre = jnp.zeros((rows, 2 * ch), F32) + bias2
        for j in range(2):
            lhs = jnp.concatenate(
                [cols[2 * p + 2 * j + t, pl.ds(b * nz, rows), :] for t in range(2) for b in range(3)], axis=1)
            pre = pre + jnp.dot(lhs, wb[j * half:(j + 1) * half, :], preferred_element_type=F32)
        into[...] = pre

    def finish(p, pre, gb):
        for t in range(2):
            u = pre[:, t * ch:(t + 1) * ch]
            sig = jax.nn.sigmoid(u)
            ob[2 * p + t] = (u * sig * mask).astype(BF)
            e = (cb[2 * p + t].astype(F32) * sig * (1.0 + u * (1.0 - sig)) * mask).astype(BF)
            gb = gb + jnp.sum(e.astype(F32), axis=0, keepdims=True)
            at = (2 * p + t + 2) * ch
            dpt[pl.ds(at if isinstance(at, int) else pl.multiple_of(at, ch), ch), :] = e.T
        return gb

    def pairs(k, gb):
        conv(2 * k + 1, preb)
        gb = finish(2 * k, prea, gb)
        conv(2 * k + 2, prea)
        return finish(2 * k + 1, preb, gb)

    conv(0, prea)
    gb = lax.fori_loop(0, nx // 4 - 1, pairs, jnp.zeros((1, ch), F32))
    conv(nx // 2 - 1, preb)
    gb = finish(nx // 2 - 2, prea, gb)
    gb = finish(nx // 2 - 1, preb, gb)
    store = pltpu.make_async_copy(ob, out_ref, ls.at[8])
    store.start()

    def grad(q0, q1, i0, i1):
        @pl.loop(i0, i1)
        def _(p):
            i = 2 * p
            lhs = jnp.concatenate(
                [dpt[pl.ds(pl.multiple_of((i + t) * ch, ch), 3 * ch), :] for t in range(2)], axis=1)
            rhs = jnp.concatenate([jnp.concatenate(
                [cols[i + t, pl.ds((o // 3) * nz, rows), (o % 3) * ch:(o % 3 + 1) * ch] for o in range(q0, q1)],
                axis=1) for t in range(2)], axis=0)
            acc[:, q0 * ch:q1 * ch] += jnp.dot(lhs, rhs, preferred_element_type=F32)

    def put(pos, tile):
        g_ref[pos // 4, pos % 4 // 2, pl.ds(2 * (pos % 2), 2)] = tile.reshape(2, 4, 16, ch)

    def tiles(q0, q1):
        for o in range(q0, q1):
            for a in range(3):
                put(o * 3 + a, acc[(2 - a) * ch:(3 - a) * ch, o * ch:(o + 1) * ch].T)

    def rcopy(src, dst, c, n, p):
        return pltpu.make_async_remote_copy(src_ref=src, dst_ref=dst, send_sem=ss.at[c, n],
                                            recv_sem=rs.at[c, n], device_id=p, device_id_type=MESH)

    def part(c):
        off, size = chunks[c]
        return pl.ds(off, size)

    def c1(c):
        return [rcopy(s1.at[part(c)], r1.at[part(c)], c, 0, peer1())]

    def c2(c):
        return [rcopy(s2.at[part(c), o], r2.at[part(c), k], c, k, p)
                for k in (1, 2, 3) for o, p in [peer2(k)]]

    def c3(c):
        return [rcopy(s3.at[part(c), o], r3.at[part(c), k], c, 3 + k, p)
                for k in (1, 2, 3) for o, p in [peer3(k)]]

    def c4(c):
        return [rcopy(s4.at[part(c), xh], s4.at[part(c), xh], c, 27 + k, p)
                for k in range(1, far) for o, p in [peer4(k)]]

    def c4in(c):
        return [rcopy(s4.at[part(c), xh], s4.at[part(c), o], c, 27 + k, p)
                for k in range(1, far) for o, p in [peer4(far - k)]]

    def c8(c):
        return [rcopy(s8.at[part(c), oh, oq], r8.at[part(c), k], c, 13 + k, p)
                for k in range(1, 8) for oh, oq, p in [peer8(k)]]

    def g3(c, inn=False):
        return [rcopy(fin.at[part(c), h, q, y], fin.at[part(c), h, q, o if inn else y], c, 6 + k, p)
                for k in (1, 2, 3) for o, p in [peer3(4 - k if inn else k)]]

    def g2(c, inn=False):
        return [rcopy(fin.at[part(c), h, q], fin.at[part(c), h, o if inn else q], c, 9 + k, p)
                for k in (1, 2, 3) for o, p in [peer2(4 - k if inn else k)]]

    def g1(c, inn=False):
        return [rcopy(fin.at[part(c), h], fin.at[part(c), 1 - h if inn else h], c, 13, peer1())]

    def g8(c, inn=False):
        return [rcopy(fin.at[part(c), h, q], fin.at[part(c), oh if inn else h, oq if inn else q],
                      c, 20 + k, p)
                for k in range(1, 8) for oh, oq, p in [peer8(8 - k if inn else k)]]

    def start(cs):
        for r in cs:
            r.start()

    def landed(cs):
        for r in cs:
            r.wait_recv()

    def st0(c):
        s1[part(c)] = g_ref[part(c), 1 - h].astype(BF)
        start(c1(c))

    def st1(c):
        landed(c1(c))
        v = g_ref[part(c), h] + r1[part(c)].astype(F32)
        a1[part(c)] = v
        s2[part(c)] = v.astype(BF)
        start(c2(c))

    def onward(c, v):
        a2[part(c)] = v
        s3[part(c)] = v.astype(BF)
        start(c3(c))

    def st2(c):
        landed(c2(c))
        v = a1[part(c), q]
        for k in (1, 2, 3):
            v = v + r2[part(c), k].astype(F32)
        onward(c, v)

    def w0(c):
        s8[part(c)] = g_ref[part(c)].astype(BF)
        start(c8(c))

    def w1(c):
        landed(c8(c))
        v = g_ref[part(c), h, q]
        for k in range(1, 8):
            v = v + r8[part(c), k].astype(F32)
        onward(c, v)

    def st3(c):
        landed(c3(c))
        v = a2[part(c), y]
        for k in (1, 2, 3):
            v = v + r3[part(c), k].astype(F32)
        if far > 1:
            s4[part(c), xh] = v.astype(BF)
            start(c4(c))
            landed(c4in(c))
            v = s4[part(c), 0].astype(F32)
            for k in range(1, far):
                v = v + s4[part(c), k].astype(F32)
        fin[part(c), h, q, y] = v.astype(BF)
        start(g3(c))

    def st4(c):
        landed(g3(c, True))
        start(g2(c))

    def st5(c):
        landed(g2(c, True))
        start(g1(c))

    def result(c):
        off, size = chunks[c]
        for pos in range(4 * off, 4 * (off + size)):
            k = pos % 4
            tile = fin[pos // 4, k // 2, 2 * (k % 2):2 * (k % 2) + 2].reshape(ch, ch)
            gw_ref[(pos % 3) * 9 + pos // 3 if pos < 27 else 27] = tile.astype(F32)

    def st6(c):
        landed(g1(c, True))
        result(c)

    def w3(c):
        landed(g3(c, True))
        start(g8(c))

    def w4(c):
        landed(g8(c, True))
        result(c)

    far_way = [st0, st1, st2, st3, st4, st5, st6]
    short_way = [w0, w1, st3, w3, w4]
    way = [far_way, far_way, short_way, short_way]
    acc[...] = jnp.zeros(acc.shape, F32)
    n = (nx + 2) // 2
    put(27, jnp.broadcast_to(gb, (ch, ch)))
    ready = {1: (0,), 2: (1,), 3: (2,), 4: (3,)}
    at = {}
    step = 0
    while step < 5 or any(v < len(way[c]) for c, v in at.items()):
        if step < 5:
            q0, q1 = 2 * step, min(2 * step + 2, 9)
            grad(q0, q1, 0, n)
            tiles(q0, q1)
        for c in sorted(at):
            if at[c] < len(way[c]):
                way[c][at[c]](c)
                at[c] += 1
        for c in ready.get(step, ()):
            way[c][0](c)
            at[c] = 1
        step += 1
    store.wait()
    for c in range(len(chunks)):
        long = way[c] is far_way
        for cs in (c3(c), c4(c), g3(c)) + ((c1(c), c2(c), g2(c), g1(c)) if long else (c8(c), g8(c))):
            for r in cs:
                r.wait_send()


def local(nsx, nsy, volume, block_active, weight, bias, cotangent):
    _, nx, ny, nz, ch = volume.shape
    blocks = block_active.shape[3]
    rows = ny * nz
    chunks = ((0, 3), (3, 1), (4, 2), (6, 1))
    far = max(nsx // 2, 1)
    anyw = pl.BlockSpec(memory_space=pltpu.HBM)
    gr = (16, ch)
    bf = lambda *dims: pltpu.VMEM(dims, BF)
    dma = pltpu.SemaphoreType.DMA
    out, gw = pl.pallas_call(
        functools.partial(layer_kernel, nsx, nsy, nz // blocks, chunks),
        out_shape=(jax.ShapeDtypeStruct((nx, rows, ch), BF),
                   jax.ShapeDtypeStruct((28, ch, ch), F32)),
        in_specs=[SM, VM, anyw, anyw, anyw], out_specs=(anyw, VM),
        scratch_shapes=[
            bf(2, ny, nz, ch), bf(2, nx, nz, ch), bf(2, ny, nz, ch), bf(2, nx + 2, nz, ch),
            bf(nx, ny, nz, ch), bf(36 * ch, 2 * ch), bf(nx, rows, ch), bf(nx, rows, ch),
            bf(nx + 2, rows + 2 * nz, 3 * ch), bf((nx + 4) * ch, rows), pltpu.VMEM((3 * ch, 9 * ch), F32),
            pltpu.VMEM((rows, 2 * ch), F32), pltpu.VMEM((rows, 2 * ch), F32),
            pltpu.VMEM((7, 2, 4, 4) + gr, F32), bf(7, 4, 4, *gr), bf(7, 4, 4, *gr),
            pltpu.VMEM((7, 4, 4) + gr, F32), bf(7, 4, 4, *gr), bf(7, 4, 4, *gr),
            pltpu.VMEM((7, 4) + gr, F32), bf(7, 4, *gr), bf(7, 4, *gr), bf(7, far, *gr),
            bf(7, 2, 4, 4, *gr), bf(7, 8, 4, *gr), bf(7, 2, 4, 4, *gr), dma((9,)), dma((8,)), dma((8,)),
            dma((len(chunks), 27 + far)), dma((len(chunks), 27 + far))],
        compiler_params=pltpu.CompilerParams(collective_id=0, has_side_effects=True,
                                             vmem_limit_bytes=40 * 2**20),
        name="layer",
    )(block_active.reshape(blocks), bias[None], volume[0],
      weight.reshape(27 * ch, ch), cotangent.reshape(nx, rows, ch))
    return (out.reshape(volume.shape), gw[:27].reshape(weight.shape), gw[27, 0])


def solution(mesh):
    tile = P("dp", "sx", "sy", None, None)
    return jax.shard_map(
        functools.partial(local, mesh.shape["sx"], mesh.shape["sy"]),
        mesh=mesh,
        in_specs=(tile, P("dp", "sx", "sy", None), P(), P(), tile),
        out_specs=(tile, P(), P()),
        check_vma=False,
    )
```
